128 devices in a mesh: tmpl: 4 (over x_hi, core), slab: 32 (over z, y, x_lo).
Axes of the slice: x: 4 (x_hi: 2, x_lo: 2; x = x_hi * 2 + x_lo), y: 4, z: 4, core: 2. Of those that a mesh axis runs over, the one named last changes fastest.
Arguments:
- hidden_section: bfloat16 [2048, 8192], P('tmpl', 'slab'), may hold values from -6 to 6
- out_grad: bfloat16 [2048, 12288], P('tmpl'), may hold values from -0.25 to 0.25
- bounds: int32 [4, 33], replicated, may hold values from 0 to 4096, as said below
- slab_slot: int32 [32], replicated, may hold values from 0 to 31, each once
- master: float32 [4096, 12288], P('tmpl', 'slab'), may hold values from -4 to 4
- moment1: float32 [4096, 12288], P('tmpl', 'slab'), may hold values from -3 to 3
- moment2: float32 [4096, 12288], P('tmpl', 'slab'), may hold values from 0.02 to 0.5
Outputs:
- section_weights: bfloat16 [32768, 12288], P(('tmpl', 'slab'))
- new_master: float32 [4096, 12288], P('tmpl', 'slab')
- new_moment1: float32 [4096, 12288], P('tmpl', 'slab')
- new_moment2: float32 [4096, 12288], P('tmpl', 'slab')
The draws below stay inside these ranges and needn't reach their ends.
Inputs may be any that keep to these rules, and one draw needn't show every extreme that they name: `bounds`: every row starts at 0 and ends at 4096; successive entries differ by 0 to 2 times 128, all multiples of 128, and every template has a section of exactly 2 slabs. `slab_slot`: each slot holds exactly one slab.
All inputs are finite; a program needn't handle non-finite values.
Results may differ from the reference program's by a relative error of at most 0.0034.
Values may be sent and summed in bfloat16 or wider, within the bound.
No kernel may reach another device: no remote copies, remote signals or barrier semaphores. Data moves between devices by JAX's collectives and lax.ppermute only.
A program may use at most 192 MiB of HBM per device.

```python
import math
import jax
import jax.numpy as jnp
from jax import lax

D = 12288
TOK = 512
SLAB_ROWS = 128
TEMPLATES = 4
SLABS = 32
WIN_ROWS = 4096
MAX_ROWS = 256


def draw_bounds(key, part):
    key = jax.random.fold_in(key, 7)

    def one_template(sub_key):
        shuffled = jax.random.permutation(sub_key, SLABS)
        rank_ids = jnp.arange(SLABS, dtype=jnp.int32)
        moved_count = SLABS // 4
        section_slabs = 1 + (rank_ids < moved_count).astype(jnp.int32) - ((rank_ids >= moved_count) & (rank_ids < 2 * moved_count)).astype(jnp.int32)
        counts = jnp.zeros((SLABS,), jnp.int32).at[shuffled].set(section_slabs)
        return jnp.concatenate([jnp.zeros((1,), jnp.int32), jnp.cumsum(counts).astype(jnp.int32) * SLAB_ROWS])
    return jax.vmap(one_template)(jax.random.split(key, TEMPLATES))


def level_of(key, extent, shards, low, top_value):
    factor_of = 1.0
    for axis_at, shards_of in shards:
        draws = jax.random.uniform(jax.random.fold_in(jax.random.fold_in(key, 6), axis_at), (shards_of,), jnp.float32, low / len(shards), top_value / len(shards))
        factor_of = factor_of * jnp.repeat(jnp.exp(draws), extent[axis_at] // shards_of).reshape((-1,) + (1,) * (len(extent) - 1 - axis_at))
    return factor_of


def scatter_about(stream_key, dims, scale, reach, cuts=(), kind=jnp.bfloat16):
    array = jax.random.normal(stream_key, dims, jnp.float32) * scale
    if len(cuts) > 0:
        array = level_of(stream_key, dims, cuts, -0.22, 0.18) * array
    return jnp.clip(array, min=-reach, max=reach).astype(kind)


def setup_inputs(seed: int = 0) -> dict:
    streams_of = jax.random.split(jax.random.key(seed), 8)
    hidden_section = scatter_about(streams_of[0], (TEMPLATES * TOK, SLABS * MAX_ROWS), 1.0, 6.0, ((0, 4), (1, 32)))
    out_grad = scatter_about(streams_of[1], (TEMPLATES * TOK, D), TOK ** -0.5, 0.25, ((0, 4),))
    bounds = draw_bounds(jax.random.fold_in(streams_of[7], 71), 0)
    slab_slot = jax.random.permutation(streams_of[3], SLABS).astype(jnp.int32)
    master = scatter_about(streams_of[4], (WIN_ROWS, D), 0.5, 4.0, ((0, 4), (1, 32)), jnp.float32)
    moment1 = scatter_about(streams_of[5], (WIN_ROWS, D), 0.3, 3.0, ((0, 4), (1, 32)), jnp.float32)
    moment2 = jnp.clip(jnp.exp(math.log(0.5) - 3.218876 * jax.random.uniform(streams_of[6], (WIN_ROWS, D), jnp.float32) ** level_of(streams_of[6], (WIN_ROWS, D), ((0, 4), (1, 32)), -0.2, 0.2)), 0.02, 0.5)
    return {"hidden_section": hidden_section, "out_grad": out_grad, "bounds": bounds, "slab_slot": slab_slot, "master": master, "moment1": moment1, "moment2": moment2}


learn_rate = 0.1
decay_rate = 0.1
beta_first = 0.9
beta_second = 0.95
adam_eps = 1e-08
step_count = 100

def adamw_update(master, moment1, moment2, gradient):
    first_moment = beta_first * moment1 + (1.0 - beta_first) * gradient
    second_moment = beta_second * moment2 + (1.0 - beta_second) * gradient * gradient
    first_hat = first_moment / (1.0 - beta_first ** step_count)
    second_hat = second_moment / (1.0 - beta_second ** step_count)
    new_master = master - learn_rate * (first_hat / (jnp.sqrt(second_hat) + adam_eps) + decay_rate * master)
    return (new_master, first_moment, second_moment)

def reference(hidden_section, out_grad, bounds, slab_slot, master, moment1, moment2):
    slab_order = jnp.argsort(slab_slot).astype(jnp.int32)
    row_ids = jnp.arange(WIN_ROWS, dtype=jnp.int32)
    global_row = (slab_order[row_ids // SLAB_ROWS] * SLAB_ROWS + row_ids % SLAB_ROWS).astype(jnp.int32)
    grad_total = jnp.zeros((WIN_ROWS, D), jnp.float32)
    for template in range(TEMPLATES):
        starts = bounds[template].astype(jnp.int32)
        section_index = lax.optimization_barrier(jnp.sum((starts[None, 1:] <= global_row[:, None]).astype(jnp.int32), axis=1)).astype(jnp.int32)
        source_row = (section_index * MAX_ROWS + global_row - starts[section_index]).astype(jnp.int32)
        acts = hidden_section[template * TOK:(template + 1) * TOK][:, source_row]
        partial_grad = jnp.dot(acts.T, out_grad[template * TOK:(template + 1) * TOK], preferred_element_type=jnp.float32).astype(jnp.bfloat16)
        grad_total = grad_total + partial_grad.astype(jnp.float32)
    gradient = grad_total / TEMPLATES
    new_master, first_moment, second_moment = adamw_update(master, moment1, moment2, gradient)
    weights = new_master.astype(jnp.bfloat16)
    padded_ids = jnp.arange(SLABS * MAX_ROWS, dtype=jnp.int32)
    owner_section = (padded_ids // MAX_ROWS).astype(jnp.int32)
    offset_rows = (padded_ids % MAX_ROWS).astype(jnp.int32)
    pieces = []
    for template in range(TEMPLATES):
        starts = bounds[template].astype(jnp.int32)
        section_first = starts[owner_section]
        section_len = starts[owner_section + 1] - section_first
        inside = offset_rows < section_len
        target_row = jnp.minimum(section_first + offset_rows, WIN_ROWS - 1).astype(jnp.int32)
        slot_row = (slab_slot[target_row // SLAB_ROWS] * SLAB_ROWS + target_row % SLAB_ROWS).astype(jnp.int32)
        pieces.append(jnp.where(inside[:, None], weights[slot_row], jnp.zeros((), jnp.bfloat16)))
    section_weights = jnp.concatenate(pieces, axis=0)
    return (section_weights, new_master, first_moment, second_moment)
```

```python
import jax
import jax.numpy as jnp
from jax import lax
from jax.experimental import pallas as pl
from jax.experimental.pallas import tpu as pltpu
from jax.sharding import Mesh, PartitionSpec as P

learn_rate = 0.1
decay_rate = 0.1
beta_first = 0.9
beta_second = 0.95
adam_eps = 1e-08
step_count = 100

TMPL = ("xh", "core")
SLAB = ("z", "y", "xl")
BF16 = jnp.bfloat16


def adamw_update(master, moment1, moment2, gradient):
    first_moment = beta_first * moment1 + (1.0 - beta_first) * gradient
    second_moment = beta_second * moment2 + (1.0 - beta_second) * gradient * gradient
    first_hat = first_moment / (1.0 - beta_first**step_count)
    second_hat = second_moment / (1.0 - beta_second**step_count)
    new_master = master - learn_rate * (
        first_hat / (jnp.sqrt(second_hat) + adam_eps) + decay_rate * master
    )
    return (new_master, first_moment, second_moment)


def shift(x, axis, step):
    n = lax.axis_size(axis)
    return lax.ppermute(x, axis, [(i, (i + step) % n) for i in range(n)])


def ring(x, axis):
    return [shift(x, axis, 1), x, shift(x, axis, -1), shift(x, axis, 2)]


def from_ring_start(x, dim, index):
    return lax.dynamic_slice_in_dim(jnp.concatenate([x, x], dim), (index + 3) % 4, 4, dim)


def swap_order(mine, other, bit):
    return jnp.stack([jnp.where(bit == 0, mine, other), jnp.where(bit == 0, other, mine)])


def to_slots(starts, slab_slot, sections, slab_rows):
    count, tokens, max_rows = sections.shape
    slots = slab_slot.shape[0]
    per = max_rows // slab_rows

    def kernel(starts_ref, slot_ref, x_ref, o_ref):
        for s in range(count):
            first = starts_ref[s] // slab_rows
            held = starts_ref[s + 1] // slab_rows - first
            for j in range(per):

                @pl.when(j < held)
                def _():
                    slot = slot_ref[jnp.minimum(first + j, slots - 1)]
                    o_ref[slot] = x_ref[s, :, j * slab_rows : (j + 1) * slab_rows]

    return pl.pallas_call(
        kernel,
        out_shape=jax.ShapeDtypeStruct((slots, tokens, slab_rows), sections.dtype),
        in_specs=[
            pl.BlockSpec(memory_space=pltpu.SMEM),
            pl.BlockSpec(memory_space=pltpu.SMEM),
            pl.BlockSpec(memory_space=pltpu.VMEM),
        ],
        out_specs=pl.BlockSpec(memory_space=pltpu.VMEM),
        name="to_slots",
    )(starts, slab_slot, sections)


def to_sections(starts, slab_slot, weights, sections, max_rows):
    slots, slab_rows, columns = weights.shape
    per = max_rows // slab_rows

    def kernel(starts_ref, slot_ref, w_ref, o_ref):
        def body(s, carry):
            first = starts_ref[s] // slab_rows
            held = starts_ref[s + 1] // slab_rows - first
            for j in range(per):
                rows = slice(j * slab_rows, (j + 1) * slab_rows)

                @pl.when(j < held)
                def _():
                    slot = slot_ref[jnp.minimum(first + j, slots - 1)]
                    o_ref[s, rows] = w_ref[slot]

                @pl.when(j >= held)
                def _():
                    o_ref[s, rows] = jnp.zeros((slab_rows, columns), weights.dtype)

            return carry

        lax.fori_loop(0, sections, body, 0)

    return pl.pallas_call(
        kernel,
        out_shape=jax.ShapeDtypeStruct((sections, max_rows, columns), weights.dtype),
        in_specs=[
            pl.BlockSpec(memory_space=pltpu.SMEM),
            pl.BlockSpec(memory_space=pltpu.SMEM),
            pl.BlockSpec(memory_space=pltpu.VMEM),
        ],
        out_specs=pl.BlockSpec(memory_space=pltpu.VMEM),
        compiler_params=pltpu.CompilerParams(vmem_limit_bytes=32 << 20),
        name="to_sections",
    )(starts, slab_slot, weights)


def per_device(hidden_section, out_grad, bounds, slab_slot, master, moment1, moment2):
    tmpl = lax.axis_index(TMPL)
    slab = lax.axis_index(SLAB)
    z, y, xl = (lax.axis_index(a) for a in SLAB)
    xh, core = (lax.axis_index(a) for a in TMPL)
    sections = lax.axis_size(SLAB)
    templates = lax.axis_size(TMPL)
    tokens, max_rows = hidden_section.shape
    own_rows, columns = master.shape
    slots = slab_slot.shape[0]
    slab_rows = own_rows * templates // slots
    part = tokens // sections
    starts = lax.dynamic_index_in_dim(bounds, tmpl, 0, keepdims=False)

    grad_own = lax.dynamic_slice_in_dim(out_grad, slab * columns, columns, 1)
    grad_pair = swap_order(grad_own, shift(grad_own, "xh", 1), xh)
    grads = swap_order(grad_pair, shift(grad_pair, "core", 1), core)
    grads = grads.transpose(1, 0, 2, 3).reshape(templates, 4, 4, 2 * part, columns)
    grads = from_ring_start(from_ring_start(grads, 1, z), 2, y)
    grads_a = grads[:2].transpose(0, 2, 1, 3, 4).reshape(2, tokens, columns)
    grads_b = grads[2:].reshape(2, tokens, columns)

    parts = lax.all_to_all(
        hidden_section.reshape(sections, part, max_rows), SLAB, 0, 0, tiled=True
    )
    in_slots = to_slots(starts, slab_slot, parts, slab_rows)
    by_quarter = (
        in_slots.reshape(templates, slots // templates, part, slab_rows)
        .transpose(0, 2, 1, 3)
        .reshape(templates, part, own_rows)
    )
    quarter = lax.all_to_all(by_quarter, TMPL, 0, 0, tiled=True)

    both = swap_order(quarter, shift(quarter, "xl", 1), xl)
    both = both.transpose(1, 0, 2, 3).reshape(templates, 1, 2 * part, own_rows)
    acts_a = jnp.concatenate(ring(both[:2], "z"), 1).reshape(2, 1, 8 * part, own_rows)
    acts_a = jnp.concatenate(ring(acts_a, "y"), 1).reshape(2, tokens, own_rows)
    acts_b = jnp.concatenate(ring(both[2:], "y"), 1).reshape(2, 1, 8 * part, own_rows)
    acts_b = jnp.concatenate(ring(acts_b, "z"), 1).reshape(2, tokens, own_rows)

    total = jnp.zeros((own_rows, columns), jnp.float32)
    for acts, some in ((acts_a, grads_a), (acts_b, grads_b)):
        for t in range(2):
            partial = lax.dot_general(
                acts[t], some[t], (((0,), (0,)), ((), ())), preferred_element_type=jnp.float32
            ).astype(BF16)
            total = total + partial.astype(jnp.float32)
    gradient = total / templates
    new_master, first_moment, second_moment = adamw_update(master, moment1, moment2, gradient)

    weights = new_master.astype(BF16)
    pair = swap_order(weights, shift(weights, "xh", 1), xh)
    full = swap_order(pair, shift(pair, "core", 1), core)
    full = full.transpose(1, 0, 2, 3).reshape(slots, slab_rows, columns)
    section_pad = to_sections(starts, slab_slot, full, sections, max_rows)
    pieces = lax.all_to_all(section_pad, SLAB, 0, 0, tiled=True)
    section_weights = pieces.transpose(1, 0, 2).reshape(max_rows, sections * columns)
    return (section_weights, new_master, first_moment, second_moment)


def solution(mesh):
    fine = Mesh(mesh.devices.reshape(2, 2, 4, 4, 2), TMPL + SLAB)
    own = P(TMPL, SLAB)
    return jax.shard_map(
        per_device,
        mesh=fine,
        in_specs=(own, P(TMPL, None), P(), P(), own, own, own),
        out_specs=(P(TMPL + SLAB, None), own, own, own),
        check_vma=False,
    )
```

```python
import jax
import jax.numpy as jnp
from jax import lax
from jax.experimental import pallas as pl
from jax.experimental.pallas import tpu as pltpu
from jax.sharding import Mesh, PartitionSpec as P

learn_rate = 0.1
decay_rate = 0.1
beta_first = 0.9
beta_second = 0.95
adam_eps = 1e-08
step_count = 100

TMPL = ("xh", "core")
SLAB = ("z", "y", "xl")
BF16 = jnp.bfloat16


def adamw_update(master, moment1, moment2, gradient):
    first_moment = beta_first * moment1 + (1.0 - beta_first) * gradient
    second_moment = beta_second * moment2 + (1.0 - beta_second) * gradient * gradient
    first_hat = first_moment / (1.0 - beta_first**step_count)
    second_hat = second_moment / (1.0 - beta_second**step_count)
    new_master = master - learn_rate * (
        first_hat / (jnp.sqrt(second_hat) + adam_eps) + decay_rate * master
    )
    return (new_master, first_moment, second_moment)


def shift(x, axis, step):
    n = lax.axis_size(axis)
    return lax.ppermute(x, axis, [(i, (i + step) % n) for i in range(n)])


def opposite(x):
    return lax.ppermute(x, ("xh", "xl"), [(0, 3), (1, 2), (2, 1), (3, 0)])


def turn(x, stage, step):
    pairs = []
    for core in range(2):
        for z in range(4):
            for y in range(4):
                to = ((z + step) % 4, y) if core == stage else (z, (y + step) % 4)
                pairs.append((core * 16 + z * 4 + y, core * 16 + to[0] * 4 + to[1]))
    return lax.ppermute(x, ("core", "z", "y"), pairs)


def ring(x, stage):
    return [turn(x, stage, 1), x, turn(x, stage, -1), turn(x, stage, 2)]


def from_ring_start(x, dim, index):
    return lax.dynamic_slice_in_dim(jnp.concatenate([x, x], dim), (index + 3) % 4, 4, dim)


def swap_order(mine, other, bit):
    return jnp.stack([jnp.where(bit == 0, mine, other), jnp.where(bit == 0, other, mine)])


def to_slots(starts, slab_slot, sections, slab_rows):
    count, tokens, max_rows = sections.shape
    slots = slab_slot.shape[0]
    per = max_rows // slab_rows

    def kernel(starts_ref, slot_ref, x_ref, o_ref):
        for s in range(count):
            first = starts_ref[s] // slab_rows
            held = starts_ref[s + 1] // slab_rows - first
            for j in range(per):

                @pl.when(j < held)
                def _():
                    slot = slot_ref[jnp.minimum(first + j, slots - 1)]
                    o_ref[slot] = x_ref[s, :, j * slab_rows : (j + 1) * slab_rows]

    return pl.pallas_call(
        kernel,
        out_shape=jax.ShapeDtypeStruct((slots, tokens, slab_rows), sections.dtype),
        in_specs=[
            pl.BlockSpec(memory_space=pltpu.SMEM),
            pl.BlockSpec(memory_space=pltpu.SMEM),
            pl.BlockSpec(memory_space=pltpu.VMEM),
        ],
        out_specs=pl.BlockSpec(memory_space=pltpu.VMEM),
        name="to_slots",
    )(starts, slab_slot, sections)


def to_sections(starts, slab_slot, weights, sections, max_rows):
    slots, slab_rows, columns = weights.shape
    per = max_rows // slab_rows

    def kernel(starts_ref, slot_ref, w_ref, o_ref):
        def body(s, carry):
            first = starts_ref[s] // slab_rows
            held = starts_ref[s + 1] // slab_rows - first
            for j in range(per):
                rows = slice(j * slab_rows, (j + 1) * slab_rows)

                @pl.when(j < held)
                def _():
                    slot = slot_ref[jnp.minimum(first + j, slots - 1)]
                    o_ref[s, rows] = w_ref[slot]

                @pl.when(j >= held)
                def _():
                    o_ref[s, rows] = jnp.zeros((slab_rows, columns), weights.dtype)

            return carry

        lax.fori_loop(0, sections, body, 0)

    return pl.pallas_call(
        kernel,
        out_shape=jax.ShapeDtypeStruct((sections, max_rows, columns), weights.dtype),
        in_specs=[
            pl.BlockSpec(memory_space=pltpu.SMEM),
            pl.BlockSpec(memory_space=pltpu.SMEM),
            pl.BlockSpec(memory_space=pltpu.VMEM),
        ],
        out_specs=pl.BlockSpec(memory_space=pltpu.VMEM),
        compiler_params=pltpu.CompilerParams(vmem_limit_bytes=32 << 20),
        name="to_sections",
    )(starts, slab_slot, weights)


def per_device(hidden_section, out_grad, bounds, slab_slot, master, moment1, moment2):
    tmpl = lax.axis_index(TMPL)
    slab = lax.axis_index(SLAB)
    z, y, xl = (lax.axis_index(a) for a in SLAB)
    xh, core = (lax.axis_index(a) for a in TMPL)
    sections = lax.axis_size(SLAB)
    templates = lax.axis_size(TMPL)
    tokens, max_rows = hidden_section.shape
    own_rows, columns = master.shape
    slots = slab_slot.shape[0]
    slab_rows = own_rows * templates // slots
    part = tokens // sections
    starts = lax.dynamic_index_in_dim(bounds, tmpl, 0, keepdims=False)

    grad_own = lax.dynamic_slice_in_dim(out_grad, slab * columns, columns, 1)
    grad_pair = swap_order(grad_own, shift(grad_own, "xh", 1), xh)
    grads = swap_order(grad_pair, shift(grad_pair, "core", 1), core)
    grads = grads.transpose(1, 0, 2, 3).reshape(templates, 4, 4, 2 * part, columns)
    grads = from_ring_start(from_ring_start(grads, 1, z), 2, y)
    grads = jnp.where(core == 0, grads.transpose(0, 2, 1, 3, 4), grads)
    grads = grads.reshape(templates, tokens, columns)

    parts = lax.all_to_all(
        hidden_section.reshape(sections, part, max_rows), SLAB, 0, 0, tiled=True
    )
    in_slots = to_slots(starts, slab_slot, parts, slab_rows)
    by_quarter = (
        in_slots.reshape(2, 2, slots // templates, part, slab_rows)
        .transpose(0, 1, 3, 2, 4)
        .reshape(2, 2, part, own_rows)
    )
    kept = lax.dynamic_index_in_dim(by_quarter, core, 1, False)
    given = lax.dynamic_index_in_dim(by_quarter, 1 - core, 1, False)
    halves = swap_order(kept, shift(given, "core", 1), core)
    near = lax.dynamic_index_in_dim(halves, xh, 1, False)
    far = lax.dynamic_index_in_dim(halves, 1 - xh, 1, False)
    near = swap_order(near, shift(near, "xl", 1), xl)
    far = swap_order(shift(far, "xh", 1), opposite(far), xl)
    both = swap_order(near, far, xh)
    both = both.transpose(0, 2, 1, 3, 4).reshape(templates, 1, 2 * part, own_rows)

    acts = jnp.concatenate(ring(both, 0), 1).reshape(templates, 1, 8 * part, own_rows)
    acts = jnp.concatenate(ring(acts, 1), 1).reshape(templates, tokens, own_rows)

    total = jnp.zeros((own_rows, columns), jnp.float32)
    for t in range(templates):
        partial = lax.dot_general(
            acts[t], grads[t], (((0,), (0,)), ((), ())), preferred_element_type=jnp.float32
        ).astype(BF16)
        total = total + partial.astype(jnp.float32)
    gradient = total / templates
    weights = adamw_update(master, moment1, moment2, gradient)[0].astype(BF16)
    weights, gradient = lax.optimization_barrier((weights, gradient))
    new_master, first_moment, second_moment = adamw_update(master, moment1, moment2, gradient)

    pair = swap_order(weights, shift(weights, "xh", 1), xh)
    full = swap_order(pair, shift(pair, "core", 1), core)
    full = full.transpose(1, 0, 2, 3).reshape(slots, slab_rows, columns)
    section_pad = to_sections(starts, slab_slot, full, sections, max_rows)
    section_weights = lax.all_to_all(
        section_pad.reshape(sections * max_rows, columns), SLAB, 0, 1, tiled=True
    )
    return (section_weights, new_master, first_moment, second_moment)


def solution(mesh):
    fine = Mesh(mesh.devices.reshape(2, 2, 4, 4, 2), TMPL + SLAB)
    own = P(TMPL, SLAB)
    return jax.shard_map(
        per_device,
        mesh=fine,
        in_specs=(own, P(TMPL, None), P(), P(), own, own, own),
        out_specs=(P(TMPL + SLAB, None), own, own, own),
        check_vma=False,
    )
```
